32 devices in a mesh: group: 2 (over y), dp: 4 (over z), tensor: 4 (over x, core).
Axes of the slice: x: 2, y: 2, z: 4, core: 2. Of those that a mesh axis runs over, the one named last changes fastest.
Arguments:
- hidden: bfloat16 [4096, 4096], P(('group', 'dp')), parts along dimension 0, may hold values from -400 to 400
- lengths: int32 [64], P(('group', 'dp')), parts along dimension 0, may hold values from 1 to 255, as said below
- assignment: int32 [64], P(('group', 'dp')), parts along dimension 0, may hold values from 0 to 3, as said below
- norm_gain: bfloat16 [4096], replicated, may hold values from 0.5 to 1.5
- q_weight: bfloat16 [4096, 2048], P(None, 'tensor'), may hold values from -0.09375 to 0.09375
- q_bias: bfloat16 [2048], P('tensor'), may hold values from -3 to 3
- k_weight: bfloat16 [4096, 512], P(None, 'tensor'), may hold values from -0.09375 to 0.09375
- k_bias: bfloat16 [512], P('tensor'), may hold values from -4 to 4
- v_weight: bfloat16 [4096, 512], P(None, 'tensor'), may hold values from -0.09375 to 0.09375
- v_bias: bfloat16 [512], P('tensor'), may hold values from -4 to 4
- prompt_keys: bfloat16 [16384, 512], P(('group', 'dp'), 'tensor'), parts along dimension 0, may hold values from -310 to 310
- prompt_values: bfloat16 [16384, 512], P(('group', 'dp'), 'tensor'), parts along dimension 0, may hold values from -6 to 6
Outputs:
- attention: bfloat16 [4096, 2048], P(('group', 'dp'), 'tensor'), parts along dimension 0
The draws below stay inside these ranges and needn't reach their ends.
There are 2 independent parts, one for each index of `group`. The reference program is written for one: setup_inputs(seed, part) draws one part's arguments, and reference() takes and returns one part's arrays. A program takes and returns all parts, laid end to end along the dimension named above; an argument that names none is the same for every part. Nothing has to cross between parts.
Inputs may be any that keep to these rules, and one draw needn't show every extreme that they name: The 8 lengths of one index of dp sum to exactly 512. `assignment`: each index of dp assigns exactly two of its responses to every index of dp, itself included, and the two have at most 256 rows together; in every draw one index of dp receives exactly 256 rows from every index of dp.
All inputs are finite; a program needn't handle non-finite values.
Results may differ from the reference program's by a relative error of at most 0.0055.
The reference program's roundings to bfloat16 on the way count: a program that leaves them out, or rounds other values in their place, can miss the bound.
Values may be sent and summed in bfloat16 or wider, within the bound.
A program may use at most 128 MiB of HBM per device.

```python
import math
import jax
import jax.numpy as jnp
from jax import lax

D = 4096
HEADS_DEV = 4
HD = 128
PLEN = 2048
TOK_DEV = 512
HEADS = 16
KV_HEADS = 4
SLOT = 256
RESP_DEV = 8
TOKENS = 2048
PROMPT_ROWS = 8192
N_DP = 4


def response_plan(key):
    subkeys = jax.random.split(key, 5)
    full_dest = jax.random.randint(subkeys[0], (), 0, N_DP)
    special = jax.random.randint(subkeys[1], (), 0, N_DP)
    others = N_DP - 1
    remaining = TOK_DEV - SLOT
    base_load = remaining // others
    extra_rows = remaining - base_load * others
    half_count = others // 2

    def one_home(row_key):
        row_subkeys = jax.random.split(row_key, 3)
        ranking = jax.random.permutation(row_subkeys[0], others)
        pair_loads = base_load + (ranking < extra_rows).astype(jnp.int32)
        for sweep_num in range(3):
            pairing = jax.random.permutation(jax.random.fold_in(row_subkeys[1], sweep_num), others)
            donors = pairing[:half_count]
            takers = pairing[half_count:2 * half_count]
            room_left = jnp.minimum(pair_loads[donors] - 2, SLOT - pair_loads[takers])
            moved_rows = jax.random.randint(jax.random.fold_in(row_subkeys[2], sweep_num), (half_count,), 0, room_left + 1)
            pair_loads = pair_loads.at[donors].add(-moved_rows).at[takers].add(moved_rows)
        return pair_loads
    others_loads = jax.vmap(one_home)(jax.random.split(subkeys[2], N_DP))
    dest_ids = jnp.arange(N_DP, dtype=jnp.int32)
    column = jnp.clip(dest_ids - (dest_ids > full_dest).astype(jnp.int32), 0, others - 1)
    pair_loads = jnp.where(dest_ids[None, :] == full_dest, SLOT, jnp.take(others_loads, column, axis=1))
    first_len = jax.random.randint(subkeys[3], (N_DP, N_DP), 1, pair_loads)
    home_ids = jnp.arange(N_DP, dtype=jnp.int32)[:, None]
    first_len = jnp.where((home_ids == special) & (dest_ids[None, :] == full_dest), SLOT - 1, first_len)
    second = pair_loads - first_len
    all_lengths = jnp.concatenate([first_len, second], axis=1)
    all_dests = jnp.broadcast_to(jnp.concatenate([dest_ids, dest_ids])[None, :], (N_DP, 2 * N_DP))
    orders = jax.vmap(lambda order_key: jax.random.permutation(order_key, 2 * N_DP))(jax.random.split(subkeys[4], N_DP))
    all_lengths = jnp.take_along_axis(all_lengths, orders, axis=1)
    all_dests = jnp.take_along_axis(all_dests, orders, axis=1)
    return (all_lengths.reshape(-1).astype(jnp.int32), all_dests.reshape(-1).astype(jnp.int32))


def draw_lengths(key, part):
    all_lengths, all_dests = response_plan(key)
    return all_lengths


def draw_assignment(key, part):
    all_lengths, all_dests = response_plan(key)
    return all_dests


def draw_hidden(key, part):
    key = jax.random.fold_in(key, 7)
    subkeys = jax.random.split(key, 4)
    row_scale = jnp.exp(jax.random.uniform(subkeys[0], (TOKENS, 1), minval=0.0, maxval=math.log(10.0)))
    col_scale = jnp.exp(jax.random.uniform(subkeys[1], (1, D), minval=0.0, maxval=math.log(10.0)))
    base_values = jnp.clip(jax.random.normal(subkeys[3], (TOKENS, D)), -4.0, 4.0)
    return (base_values * row_scale * col_scale).astype(jnp.bfloat16)


def draw_prompt_keys(key, part):
    key = jax.random.fold_in(key, 13)
    subkeys = jax.random.split(key, 1)
    key_width = KV_HEADS * HD
    cached = 0.5 * jnp.clip(jax.random.normal(subkeys[0], (N_DP * PLEN, key_width)), -4.0, 4.0)
    return cached.astype(jnp.bfloat16)


def block_levels(key, dims, cuts, smallest, high):
    level, own = 1.0, jax.random.fold_in(key, 6)
    for dim, parts in cuts:
        steps = jnp.exp(jax.random.uniform(jax.random.fold_in(own, dim), (parts,), jnp.float32, smallest / len(cuts), high / len(cuts)))
        level = level * jnp.repeat(steps, dims[dim] // parts).reshape([-1 if axis == dim else 1 for axis in range(len(dims))])
    return level


def gaussian(own_key, shape, deviation, most, cuts=(), kind=jnp.bfloat16):
    drawn = jax.random.normal(own_key, shape, jnp.float32) * deviation
    if len(cuts) > 0:
        drawn = block_levels(own_key, shape, cuts, -0.22, 0.18) * drawn
    return jnp.clip(drawn, min=-most, max=most).astype(kind)


def setup_inputs(seed: int = 0, part: int = 0) -> dict:
    keys = jax.random.split(jax.random.key(seed), 13)
    own_keys = jax.random.split(jax.random.fold_in(keys[12], part), 13)
    return {
        "hidden": draw_hidden(jax.random.fold_in(jax.random.fold_in(keys[12], part), 71), part),
        "lengths": draw_lengths(jax.random.fold_in(jax.random.fold_in(keys[12], part), 71), part),
        "assignment": draw_assignment(jax.random.fold_in(jax.random.fold_in(keys[12], part), 71), part),
        "norm_gain": jnp.clip(jax.random.uniform(keys[3], (D,), jnp.float32, 0.5, 1.5), 0.5, 1.5).astype(jnp.bfloat16),
        "q_weight": gaussian(keys[4], (D, HEADS * HD), D ** -0.5, 0.09375, ((1, 4),)),
        "q_bias": gaussian(keys[5], (HEADS * HD,), 0.5, 3.0, ((0, 4),)),
        "k_weight": gaussian(keys[6], (D, KV_HEADS * HD), D ** -0.5, 0.09375, ((1, 4),)),
        "k_bias": gaussian(keys[7], (KV_HEADS * HD,), 1.0, 4.0, ((0, 4),)),
        "v_weight": gaussian(keys[8], (D, KV_HEADS * HD), D ** -0.5, 0.09375, ((1, 4),)),
        "v_bias": gaussian(keys[9], (KV_HEADS * HD,), 1.0, 4.0, ((0, 4),)),
        "prompt_keys": draw_prompt_keys(jax.random.fold_in(jax.random.fold_in(keys[12], part), 71), part),
        "prompt_values": gaussian(own_keys[11], (PROMPT_ROWS, KV_HEADS * HD), 1.0, 6.0, ((0, 4), (1, 4))),
    }


rope_base = 1000000.0
norm_eps = 1e-06

def rotate(lin_values, position, head_size):
    half_size = head_size // 2
    freqs = rope_base ** (-(jnp.arange(half_size, dtype=jnp.float32) * 2.0) / head_size)
    angles = position.astype(jnp.float32)[:, None] * freqs[None, :]
    cosine = jnp.cos(angles)[:, None, :]
    sine = jnp.sin(angles)[:, None, :]
    first_half = lin_values[..., :half_size]
    second_half = lin_values[..., half_size:]
    return jnp.concatenate([first_half * cosine - second_half * sine, second_half * cosine + first_half * sine], axis=-1)

def response_tables(resp_lengths, resp_dest):
    ordinal = jnp.arange(resp_lengths.shape[0], dtype=jnp.int32)
    starts = (jnp.cumsum(resp_lengths) - resp_lengths).astype(jnp.int32)
    same_dest = resp_dest[:, None] == resp_dest[None, :]
    earlier = ordinal[None, :] < ordinal[:, None]
    offsets = lax.optimization_barrier(jnp.sum(jnp.where(same_dest & earlier, resp_lengths[None, :], 0), axis=1)).astype(jnp.int32)
    return (starts, offsets)

def slot_owner(resp_lengths, resp_dest, slot_dest, within):
    starts, offsets = response_tables(resp_lengths, resp_dest)
    ordinal = jnp.arange(resp_lengths.shape[0], dtype=jnp.int32)
    matches = (resp_dest[None, :] == slot_dest[:, None]) & (offsets[None, :] <= within[:, None]) & (within[:, None] < (offsets + resp_lengths)[None, :])
    occupied = jnp.any(matches, axis=1)
    owner_id = jnp.where(occupied, lax.optimization_barrier(jnp.sum(jnp.where(matches, ordinal[None, :], 0), axis=1)), -1).astype(jnp.int32)
    place_in = (within - lax.optimization_barrier(jnp.sum(jnp.where(matches, offsets[None, :], 0), axis=1))).astype(jnp.int32)
    home_row = (lax.optimization_barrier(jnp.sum(jnp.where(matches, starts[None, :], 0), axis=1)) + place_in).astype(jnp.int32)
    return (owner_id, place_in, home_row, occupied)

def home_slots(resp_lengths, resp_dest, slot_size, total_rows):
    starts, offsets = response_tables(resp_lengths, resp_dest)
    row_ids = jnp.arange(total_rows, dtype=jnp.int32)
    member = (row_ids[:, None] >= starts[None, :]) & (row_ids[:, None] < (starts + resp_lengths)[None, :])
    place_in = (row_ids - lax.optimization_barrier(jnp.sum(jnp.where(member, starts[None, :], 0), axis=1))).astype(jnp.int32)
    target = (lax.optimization_barrier(jnp.sum(jnp.where(member, (resp_dest * slot_size + offsets)[None, :], 0), axis=1)) + place_in).astype(jnp.int32)
    return (place_in, target)

def reference(hidden, lengths, assignment, norm_gain, q_weight, q_bias, k_weight, k_bias, v_weight, v_bias, prompt_keys, prompt_values):
    widened = hidden.astype(jnp.float32)
    scale_row = lax.rsqrt(lax.optimization_barrier(jnp.mean(widened * widened, axis=1, keepdims=True)) + norm_eps)
    normed = (widened * scale_row * norm_gain.astype(jnp.float32)).astype(jnp.bfloat16)
    q_lin = jnp.dot(normed, q_weight, preferred_element_type=jnp.float32) + q_bias.astype(jnp.float32)
    k_lin = jnp.dot(normed, k_weight, preferred_element_type=jnp.float32) + k_bias.astype(jnp.float32)
    values = (jnp.dot(normed, v_weight, preferred_element_type=jnp.float32) + v_bias.astype(jnp.float32)).astype(jnp.bfloat16)
    values = values.reshape(TOKENS, KV_HEADS, HD)
    home_len = lengths.reshape(N_DP, RESP_DEV)
    home_dest = assignment.reshape(N_DP, RESP_DEV)

    def home_table(resp_lengths, resp_dest):
        return home_slots(resp_lengths, resp_dest, SLOT, TOK_DEV)
    home_place, home_target = jax.vmap(home_table)(home_len, home_dest)
    position = (PLEN + home_place).reshape(TOKENS)
    queries = rotate(q_lin.reshape(TOKENS, HEADS, HD), position, HD).astype(jnp.bfloat16)
    keys_rot = rotate(k_lin.reshape(TOKENS, KV_HEADS, HD), position, HD).astype(jnp.bfloat16)
    slot_index = jnp.arange(N_DP * SLOT, dtype=jnp.int32)

    def send_table(resp_lengths, resp_dest):
        return slot_owner(resp_lengths, resp_dest, slot_index // SLOT, slot_index % SLOT)
    owner_id, slot_place, home_row, occupied = jax.vmap(send_table)(home_len, home_dest)
    global_row = home_row + jnp.arange(N_DP, dtype=jnp.int32)[:, None] * TOK_DEV
    pair_rows = global_row.reshape(N_DP * N_DP, SLOT)
    pair_tags = owner_id.reshape(N_DP * N_DP, SLOT)
    pair_place = slot_place.reshape(N_DP * N_DP, SLOT)
    pair_dest = jnp.tile(jnp.arange(N_DP, dtype=jnp.int32), N_DP)
    cached_keys = prompt_keys.reshape(N_DP, PLEN, KV_HEADS, HD)
    cached_values = prompt_values.reshape(N_DP, PLEN, KV_HEADS, HD)
    score_scale = HD ** (-0.5)

    def attend(pair_data):
        slot_rows, slot_tags, slot_places, destination = pair_data
        q_pair = jnp.take(queries, slot_rows, axis=0).astype(jnp.float32).reshape(SLOT, KV_HEADS, HEADS_DEV, HD)
        k_pair = jnp.take(keys_rot, slot_rows, axis=0).astype(jnp.float32)
        v_pair = jnp.take(values, slot_rows, axis=0).astype(jnp.float32)
        k_cache = jnp.take(cached_keys, destination, axis=0).astype(jnp.float32)
        v_cache = jnp.take(cached_values, destination, axis=0).astype(jnp.float32)
        cached_scores = jnp.einsum('skgd,pkd->kgsp', q_pair, k_cache) * score_scale
        own_scores = jnp.einsum('skgd,tkd->kgst', q_pair, k_pair) * score_scale
        allowed = (slot_tags[:, None] == slot_tags[None, :]) & (slot_places[None, :] <= slot_places[:, None])
        own_scores = jnp.where(allowed, own_scores, -jnp.inf)
        peak_score = jnp.maximum(lax.optimization_barrier(jnp.max(cached_scores, axis=3, keepdims=True)), lax.optimization_barrier(jnp.max(own_scores, axis=3, keepdims=True)))
        cached_w = jnp.exp(cached_scores - peak_score)
        own_w = jnp.exp(own_scores - peak_score)
        weight_sum = lax.optimization_barrier(jnp.sum(cached_w, axis=3)) + lax.optimization_barrier(jnp.sum(own_w, axis=3))
        cached_r = lax.optimization_barrier(cached_w.astype(jnp.bfloat16)).astype(jnp.float32)
        own_r = lax.optimization_barrier(own_w.astype(jnp.bfloat16)).astype(jnp.float32)
        summed = jnp.einsum('kgsp,pkd->skgd', cached_r, v_cache) + jnp.einsum('kgst,tkd->skgd', own_r, v_pair)
        result_pair = summed / jnp.transpose(weight_sum, (2, 0, 1))[..., None]
        return result_pair.astype(jnp.bfloat16).reshape(SLOT, HEADS * HD)
    pair_out = lax.map(attend, (pair_rows, pair_tags, pair_place, pair_dest))
    per_home = pair_out.reshape(N_DP, N_DP * SLOT, HEADS * HD)

    def unpack(home_block, home_index):
        return jnp.take(home_block, home_index, axis=0)
    result = jax.vmap(unpack)(per_home, home_target)
    return result.reshape(TOKENS, HEADS * HD)
```

```python
import functools
import math

import jax
import jax.numpy as jnp
from jax import lax
from jax.experimental import pallas as pl
from jax.experimental.pallas import tpu as pltpu
from jax.sharding import PartitionSpec as P

rope_base = 1000000.0
norm_eps = 1e-06
F32, BF16 = jnp.float32, jnp.bfloat16
MESH = pl.DeviceIdType.MESH
NT = (((1,), (1,)), ((), ()))


def kernel(
    n,
    len_ref,
    dest_ref,
    hidden_hbm,
    gain_ref,
    qw_hbm,
    qb_ref,
    kw_hbm,
    kb_ref,
    vw_hbm,
    vb_ref,
    pk_hbm,
    pv_hbm,
    table_ref,
    out_ref,
    hidden,
    normed,
    qw,
    kvw,
    pk,
    pv,
    queries,
    q_out,
    q_in,
    o_out,
    o_in,
    s_out,
    s_in,
    own_acc,
    own_stat,
    load_sem,
    q_send,
    q_recv,
    o_send,
    o_recv,
    s_send,
    s_recv,
):
    rows, feats = hidden.shape
    pairs, _, _, slot, hd = q_out.shape
    responses = len_ref.shape[0]
    factor = hd**-0.5 * math.log2(math.e)
    me = lax.axis_index("dp")

    loads = [
        pltpu.make_async_copy(hidden_hbm, hidden, load_sem.at[0]),
        pltpu.make_async_copy(qw_hbm, qw, load_sem.at[1]),
        pltpu.make_async_copy(kw_hbm, kvw.at[0], load_sem.at[2]),
        pltpu.make_async_copy(vw_hbm, kvw.at[1], load_sem.at[3]),
        pltpu.make_async_copy(pk_hbm, pk, load_sem.at[4]),
        pltpu.make_async_copy(pv_hbm, pv, load_sem.at[5]),
    ]
    for load in loads:
        load.start()

    barrier = pltpu.get_barrier_semaphore()
    for k in range(1, n):
        pl.semaphore_signal(
            barrier, inc=1, device_id={"dp": lax.rem(me + k, n)}, device_id_type=MESH
        )

    lengths = [len_ref[r] for r in range(responses)]
    dests = [dest_ref[r] for r in range(responses)]
    starts, shifts = [], []
    start = jnp.int32(0)
    for r in range(responses):
        offset = jnp.int32(0)
        for e in range(r):
            offset = offset + jnp.where(dests[e] == dests[r], lengths[e], 0)
        starts.append(start)
        shifts.append(dests[r] * slot + offset - start)
        start = start + lengths[r]

    def route(index):
        first = jnp.zeros_like(index)
        shift = jnp.zeros_like(index)
        for r in range(responses):
            reached = index >= starts[r]
            first = jnp.where(reached, starts[r], first)
            shift = jnp.where(reached, shifts[r], shift)
        return first, index + shift

    row_col = lax.broadcasted_iota(jnp.int32, (rows, 1), 0)
    first_col, target_col = route(row_col)
    _, target_row = route(lax.broadcasted_iota(jnp.int32, (1, rows), 1))

    spans = table_ref.shape[0]
    place_hot = (
        lax.broadcasted_iota(jnp.int32, (rows, spans), 1) == row_col - first_col
    ).astype(F32)
    turns = jnp.dot(
        place_hot, table_ref[...], precision=lax.Precision.HIGHEST, preferred_element_type=F32
    )
    cosine, sine = turns[:, :hd], turns[:, hd:]

    def rope(block):
        return (block * cosine + pltpu.roll(block, hd // 2, 1) * sine).astype(BF16)

    loads[0].wait()
    gain = gain_ref[...].astype(F32)
    step_rows = min(64, rows)

    def norm_step(i, carry):
        at = pl.ds(pl.multiple_of(i * step_rows, step_rows), step_rows)
        wide = hidden[at, :].astype(F32)
        scale = lax.rsqrt(jnp.mean(wide * wide, axis=1, keepdims=True) + norm_eps)
        normed[at, :] = (wide * scale * gain).astype(BF16)
        return carry

    lax.fori_loop(0, rows // step_rows, norm_step, 0)

    def q_copy(p, k):
        return pltpu.make_async_remote_copy(
            src_ref=q_out.at[p, k],
            dst_ref=q_in.at[p, k],
            send_sem=q_send.at[p, k],
            recv_sem=q_recv.at[p, k],
            device_id={"dp": lax.rem(me + k, n)},
            device_id_type=MESH,
        )

    def o_copy(p, k):
        return pltpu.make_async_remote_copy(
            src_ref=o_out.at[p, k],
            dst_ref=o_in.at[p, k],
            send_sem=o_send.at[p, k],
            recv_sem=o_recv.at[p, k],
            device_id={"dp": lax.rem(me - k + n, n)},
            device_id_type=MESH,
        )

    def s_copy(p, k):
        return pltpu.make_async_remote_copy(
            src_ref=s_out.at[p, k],
            dst_ref=s_in.at[p, k],
            send_sem=s_send.at[p, k],
            recv_sem=s_recv.at[p, k],
            device_id={"dp": lax.rem(me - k + n, n)},
            device_id_type=MESH,
        )

    order = [k for k in range(1, n) if k % 2 == 0] + [k for k in range(1, n) if k % 2] + [0]
    loads[1].wait()
    for p in range(pairs):
        cols = slice(p * 2 * hd, (p + 1) * 2 * hd)
        lin = jnp.dot(normed[...], qw[:, cols], preferred_element_type=F32)
        lin = lin + qb_ref[:, cols].astype(F32)
        both = jnp.concatenate([rope(lin[:, :hd]), rope(lin[:, hd:])], axis=1)
        queries[2 * p] = both[:, :hd]
        queries[2 * p + 1] = both[:, hd:]
        if p == 0:
            pl.semaphore_wait(barrier, n - 1)
        for k in order:
            base = lax.rem(me + k, n) * slot
            hot = lax.broadcasted_iota(jnp.int32, (slot, rows), 0) + base == target_row
            sent = jnp.dot(hot.astype(BF16), both, preferred_element_type=F32).astype(BF16)
            q_out[p, k, 0] = sent[:, :hd]
            q_out[p, k, 1] = sent[:, hd:]
            if k:
                q_copy(p, k).start()

    loads[2].wait()
    loads[3].wait()
    k_lin = jnp.dot(normed[...], kvw[0], preferred_element_type=F32) + kb_ref[...].astype(F32)
    keys = rope(k_lin)
    v_lin = jnp.dot(normed[...], kvw[1], preferred_element_type=F32) + vb_ref[...].astype(F32)
    values = v_lin.astype(BF16)
    col_row = lax.broadcasted_iota(jnp.int32, (rows, rows), 1)
    allowed = (col_row >= first_col) & (col_row <= row_col)
    stat_lane = lax.broadcasted_iota(jnp.int32, (rows, 128), 1)
    for h in range(2 * pairs):
        scores = lax.dot_general(queries[h], keys, NT, preferred_element_type=F32)
        scores = jnp.where(allowed, scores, -jnp.inf)
        peak = jnp.max(scores, axis=1, keepdims=True)
        weights = jnp.exp2((scores - peak) * factor)
        total = jnp.sum(weights, axis=1, keepdims=True)
        own_acc[h] = jnp.dot(weights.astype(BF16), values, preferred_element_type=F32)
        own_stat[h] = jnp.where(stat_lane == 0, peak, total)

    loads[4].wait()
    loads[5].wait()
    eye = (
        lax.broadcasted_iota(jnp.int32, (8, 128), 0) == lax.broadcasted_iota(jnp.int32, (8, 128), 1)
    ).astype(F32)
    lane = lax.broadcasted_iota(jnp.int32, (slot, 128), 1)

    def cached(p, k, source, o_to, s_to):
        stat = jnp.zeros((slot, 128), F32)
        for h in range(2):
            scores = lax.dot_general(source[p, k, h], pk[...], NT, preferred_element_type=F32)
            peak = jnp.max(scores, axis=1, keepdims=True)
            weights = jnp.exp2((scores - peak) * factor)
            total = jnp.sum(weights, axis=1, keepdims=True)
            summed = jnp.dot(weights.astype(BF16), pv[...], preferred_element_type=F32)
            o_to[p, k, h] = (summed / total).astype(BF16)
            stat = jnp.where(lane == 2 * h, peak, jnp.where(lane == 2 * h + 1, total, stat))
        s_to[p, k] = lax.dot_general(
            eye, stat, NT, precision=lax.Precision.HIGHEST, preferred_element_type=F32
        )

    def own_step(p, carry):
        cached(p, 0, q_out, o_in, s_in)
        return carry

    lax.fori_loop(0, pairs, own_step, 0)

    def away_step(i, carry):
        p = i // (n - 1)
        k = i % (n - 1) + 1
        q_copy(p, k).wait_recv()
        cached(p, k, q_in, o_out, s_out)
        o_copy(p, k).start()
        s_copy(p, k).start()
        return carry

    lax.fori_loop(0, pairs * (n - 1), away_step, 0)

    for p in range(pairs):
        gathered = jnp.zeros((rows, 2 * hd), F32)
        stat = jnp.zeros((rows, 8), F32)
        for k in [0] + list(range(1, n)):
            if k:
                o_copy(p, k).wait_recv()
                s_copy(p, k).wait_recv()
            base = lax.rem(me + k, n) * slot
            hot = lax.broadcasted_iota(jnp.int32, (rows, slot), 1) + base == target_col
            block = jnp.concatenate([o_in[p, k, 0], o_in[p, k, 1]], axis=1)
            gathered += jnp.dot(hot.astype(BF16), block, preferred_element_type=F32)
            stat += lax.dot_general(
                hot.astype(F32),
                s_in[p, k],
                NT,
                precision=lax.Precision.HIGHEST,
                preferred_element_type=F32,
            )
        for h in range(2):
            head = 2 * p + h
            peak, total = stat[:, 2 * h : 2 * h + 1], stat[:, 2 * h + 1 : 2 * h + 2]
            own_peak, own_total = own_stat[head][:, 0:1], own_stat[head][:, 1:2]
            top = jnp.maximum(peak, own_peak)
            far = jnp.exp2((peak - top) * factor) * total
            near = jnp.exp2((own_peak - top) * factor)
            mixed = gathered[:, h * hd : (h + 1) * hd] * far + own_acc[head] * near
            out_ref[:, head * hd : (head + 1) * hd] = (
                mixed / (far + near * own_total)
            ).astype(BF16)

    for p in range(pairs):
        for k in range(1, n):
            q_copy(p, k).wait_send()
            o_copy(p, k).wait_send()
            s_copy(p, k).wait_send()


def local(
    hidden,
    lengths,
    assignment,
    norm_gain,
    q_weight,
    q_bias,
    k_weight,
    k_bias,
    v_weight,
    v_bias,
    prompt_keys,
    prompt_values,
):
    n = lax.axis_size("dp")
    rows, feats = hidden.shape
    slot = 2 * rows // n
    hd = k_weight.shape[1]
    cols = q_weight.shape[1]
    pairs = cols // hd // 2
    plen = prompt_keys.shape[0]
    half = hd // 2
    freqs = rope_base ** (-(jnp.arange(half, dtype=F32) * 2.0) / hd)
    position = plen + jnp.arange(slot, dtype=jnp.int32)
    angles = position.astype(F32)[:, None] * freqs[None, :]
    cosine, sine = jnp.cos(angles), jnp.sin(angles)
    table = jnp.concatenate([cosine, cosine, -sine, sine], axis=1)
    smem = pl.BlockSpec(memory_space=pltpu.SMEM)
    vmem = pl.BlockSpec(memory_space=pltpu.VMEM)
    hbm = pl.BlockSpec(memory_space=pl.ANY)
    dma = pltpu.SemaphoreType.DMA
    flops = 2 * rows * feats * (cols + 2 * hd) + 8 * rows * cols * plen
    return pl.pallas_call(
        functools.partial(kernel, n),
        out_shape=jax.ShapeDtypeStruct((rows, cols), BF16),
        in_specs=[smem, smem, hbm, vmem, hbm, vmem, hbm, vmem, hbm, vmem, hbm, hbm, vmem],
        out_specs=vmem,
        scratch_shapes=[
            pltpu.VMEM((rows, feats), BF16),
            pltpu.VMEM((rows, feats), BF16),
            pltpu.VMEM((feats, cols), BF16),
            pltpu.VMEM((2, feats, hd), BF16),
            pltpu.VMEM((plen, hd), BF16),
            pltpu.VMEM((plen, hd), BF16),
            pltpu.VMEM((2 * pairs, rows, hd), BF16),
            pltpu.VMEM((pairs, n, 2, slot, hd), BF16),
            pltpu.VMEM((pairs, n, 2, slot, hd), BF16),
            pltpu.VMEM((pairs, n, 2, slot, hd), BF16),
            pltpu.VMEM((pairs, n, 2, slot, hd), BF16),
            pltpu.VMEM((pairs, n, 8, slot), F32),
            pltpu.VMEM((pairs, n, 8, slot), F32),
            pltpu.VMEM((2 * pairs, rows, hd), F32),
            pltpu.VMEM((2 * pairs, rows, 128), F32),
            dma((6,)),
            dma((pairs, n)),
            dma((pairs, n)),
            dma((pairs, n)),
            dma((pairs, n)),
            dma((pairs, n)),
            dma((pairs, n)),
        ],
        compiler_params=pltpu.CompilerParams(
            collective_id=0, has_side_effects=True, vmem_limit_bytes=56 * 1024 * 1024
        ),
        cost_estimate=pl.CostEstimate(
            flops=flops, bytes_accessed=rows * feats * 6, transcendentals=2 * rows * plen * 4
        ),
    )(
        lengths,
        assignment,
        hidden,
        norm_gain.reshape(1, -1),
        q_weight,
        q_bias.reshape(1, -1),
        k_weight,
        k_bias.reshape(1, -1),
        v_weight,
        v_bias.reshape(1, -1),
        prompt_keys,
        prompt_values,
        table,
    )


def solution(mesh):
    in_specs = (
        P(("group", "dp"), None),
        P(("group", "dp")),
        P(("group", "dp")),
        P(),
        P(None, "tensor"),
        P("tensor"),
        P(None, "tensor"),
        P("tensor"),
        P(None, "tensor"),
        P("tensor"),
        P(("group", "dp"), "tensor"),
        P(("group", "dp"), "tensor"),
    )
    out_specs = P(("group", "dp"), "tensor")
    return jax.shard_map(
        local, mesh=mesh, in_specs=in_specs, out_specs=out_specs, check_vma=False
    )
```

```python
import functools
import math

import jax
import jax.numpy as jnp
from jax import lax
from jax.experimental import pallas as pl
from jax.experimental.pallas import tpu as pltpu
from jax.sharding import PartitionSpec as P

rope_base = 1000000.0
norm_eps = 1e-06
F32, BF16 = jnp.float32, jnp.bfloat16
MESH = pl.DeviceIdType.MESH
NT = (((1,), (1,)), ((), ()))


def kernel(
    n,
    len_ref,
    dest_ref,
    hidden_hbm,
    gain_ref,
    qw_hbm,
    qb_ref,
    kw_hbm,
    kb_ref,
    vw_hbm,
    vb_ref,
    pk_hbm,
    pv_hbm,
    cos_ref,
    sin_ref,
    out_ref,
    hidden,
    normed,
    qw,
    kvw,
    pk,
    pv,
    queries,
    q_out,
    q_in,
    o_out,
    o_in,
    s_out,
    s_in,
    own_acc,
    own_stat,
    load_sem,
    hidden_sem,
    qw_sem,
    q_send,
    q_recv,
    o_send,
    o_recv,
    s_send,
    s_recv,
):
    rows, feats = hidden.shape
    pairs, _, _, slot, hd = q_out.shape
    responses = len_ref.shape[0]
    factor = hd**-0.5 * math.log2(math.e)
    me = lax.axis_index("dp")

    chunk = min(128, rows)
    chunks = [slice(c * chunk, (c + 1) * chunk) for c in range(rows // chunk)]
    hidden_loads = [
        pltpu.make_async_copy(hidden_hbm.at[at], hidden.at[at], hidden_sem.at[c])
        for c, at in enumerate(chunks)
    ]
    pair_cols = [slice(p * 2 * hd, (p + 1) * 2 * hd) for p in range(pairs)]
    qw_loads = [
        pltpu.make_async_copy(qw_hbm.at[:, at], qw.at[:, at], qw_sem.at[p])
        for p, at in enumerate(pair_cols)
    ]
    loads = qw_loads[1:] + [
        pltpu.make_async_copy(kw_hbm, kvw.at[0], load_sem.at[0]),
        pltpu.make_async_copy(vw_hbm, kvw.at[1], load_sem.at[1]),
        pltpu.make_async_copy(pk_hbm, pk, load_sem.at[2]),
        pltpu.make_async_copy(pv_hbm, pv, load_sem.at[3]),
    ]
    for load in hidden_loads + qw_loads[:1]:
        load.start()

    barrier = pltpu.get_barrier_semaphore()
    for k in range(1, n):
        pl.semaphore_signal(
            barrier, inc=1, device_id={"dp": lax.rem(me + k, n)}, device_id_type=MESH
        )

    paired = n & (n - 1) == 0 and n <= 4

    def toggled(k):
        index = me
        for bit in (1, 2):
            if k & bit:
                index = index + bit - 2 * bit * ((me // bit) % 2)
        return index

    def target_of(k):
        return toggled(k) if paired else lax.rem(me + k, n)

    def origin_of(k):
        return toggled(k) if paired else lax.rem(me - k + n, n)

    lengths = [len_ref[r] for r in range(responses)]
    dests = [dest_ref[r] for r in range(responses)]
    starts, shifts = [], []
    start = jnp.int32(0)
    for r in range(responses):
        offset = jnp.int32(0)
        for e in range(r):
            offset = offset + jnp.where(dests[e] == dests[r], lengths[e], 0)
        starts.append(start)
        shifts.append(dests[r] * slot + offset - start)
        start = start + lengths[r]

    def route(index):
        first = jnp.zeros_like(index)
        shift = jnp.zeros_like(index)
        for r in range(responses):
            reached = index >= starts[r]
            first = jnp.where(reached, starts[r], first)
            shift = jnp.where(reached, shifts[r], shift)
        return first, index + shift

    row_col = lax.broadcasted_iota(jnp.int32, (rows, 1), 0)
    first_col, target_col = route(row_col)
    _, target_row = route(lax.broadcasted_iota(jnp.int32, (1, rows), 1))

    spans = cos_ref.shape[0]
    place_hot = (
        lax.broadcasted_iota(jnp.int32, (rows, spans), 1) == row_col - first_col
    ).astype(F32)
    def turn(ref):
        return jnp.dot(
            place_hot, ref[...], precision=lax.Precision.HIGHEST, preferred_element_type=F32
        )

    cos_half, sin_half = turn(cos_ref), turn(sin_ref)
    cosine = jnp.concatenate([cos_half, cos_half], axis=1)
    sine = jnp.concatenate([-sin_half, sin_half], axis=1)

    def rope(block):
        return (block * cosine + pltpu.roll(block, hd // 2, 1) * sine).astype(BF16)

    gain = gain_ref[...].astype(F32).reshape(1, feats)
    q_bias = qb_ref[...].astype(F32).reshape(1, 2 * pairs * hd)
    k_bias = kb_ref[...].astype(F32).reshape(1, hd)
    v_bias = vb_ref[...].astype(F32).reshape(1, hd)
    first_lin = []
    for c, at in enumerate(chunks):
        hidden_loads[c].wait()
        wide = hidden[at, :].astype(F32)
        scale = lax.rsqrt(jnp.mean(wide * wide, axis=1, keepdims=True) + norm_eps)
        normed[at, :] = (wide * scale * gain).astype(BF16)
        if c == 0:
            qw_loads[0].wait()
        first_lin.append(
            jnp.dot(normed[at, :], qw[:, pair_cols[0]], preferred_element_type=F32)
        )
    for load in loads:
        load.start()

    def q_copy(p, k):
        return pltpu.make_async_remote_copy(
            src_ref=q_out.at[p, k],
            dst_ref=q_in.at[p, k],
            send_sem=q_send.at[p, k],
            recv_sem=q_recv.at[p, k],
            device_id={"dp": target_of(k)},
            device_id_type=MESH,
        )

    def o_copy(p, k):
        return pltpu.make_async_remote_copy(
            src_ref=o_out.at[p, k],
            dst_ref=o_in.at[p, k],
            send_sem=o_send.at[p, k],
            recv_sem=o_recv.at[p, k],
            device_id={"dp": origin_of(k)},
            device_id_type=MESH,
        )

    def s_copy(p, k):
        return pltpu.make_async_remote_copy(
            src_ref=s_out.at[p, k],
            dst_ref=s_in.at[p, k],
            send_sem=s_send.at[p, k],
            recv_sem=s_recv.at[p, k],
            device_id={"dp": origin_of(k)},
            device_id_type=MESH,
        )

    order = ([2, 3, 1] if paired and n == 4 else list(range(1, n))) + [0]
    for p in range(pairs):
        cols = pair_cols[p]
        if p:
            qw_loads[p].wait()
            lin = jnp.dot(normed[...], qw[:, cols], preferred_element_type=F32)
        else:
            lin = jnp.concatenate(first_lin, axis=0)
        lin = lin + q_bias[:, cols]
        both = jnp.concatenate([rope(lin[:, :hd]), rope(lin[:, hd:])], axis=1)
        queries[2 * p] = both[:, :hd]
        queries[2 * p + 1] = both[:, hd:]
        if p == 0:
            pl.semaphore_wait(barrier, n - 1)
        for k in order:
            base = target_of(k) * slot
            hot = lax.broadcasted_iota(jnp.int32, (slot, rows), 0) + base == target_row
            sent = jnp.dot(hot.astype(BF16), both, preferred_element_type=F32).astype(BF16)
            q_out[p, k, 0] = sent[:, :hd]
            q_out[p, k, 1] = sent[:, hd:]
            if k:
                q_copy(p, k).start()

    loads = loads[pairs - 1 :]
    loads[0].wait()
    loads[1].wait()
    k_lin = jnp.dot(normed[...], kvw[0], preferred_element_type=F32) + k_bias
    keys = rope(k_lin)
    v_lin = jnp.dot(normed[...], kvw[1], preferred_element_type=F32) + v_bias
    values = v_lin.astype(BF16)
    col_row = lax.broadcasted_iota(jnp.int32, (rows, rows), 1)
    allowed = (col_row >= first_col) & (col_row <= row_col)
    stat_lane = lax.broadcasted_iota(jnp.int32, (rows, 128), 1)
    for h in range(2 * pairs):
        scores = lax.dot_general(queries[h], keys, NT, preferred_element_type=F32)
        scores = jnp.where(allowed, scores, -jnp.inf)
        peak = jnp.max(scores, axis=1, keepdims=True)
        weights = jnp.exp2((scores - peak) * factor)
        total = jnp.sum(weights, axis=1, keepdims=True)
        own_acc[h] = jnp.dot(weights.astype(BF16), values, preferred_element_type=F32)
        own_stat[h] = jnp.where(stat_lane == 0, peak, total)

    loads[2].wait()
    loads[3].wait()
    eye = (
        lax.broadcasted_iota(jnp.int32, (8, 128), 0) == lax.broadcasted_iota(jnp.int32, (8, 128), 1)
    ).astype(F32)
    lane = lax.broadcasted_iota(jnp.int32, (slot, 128), 1)

    def cached(p, k, source, o_to, s_to):
        stat = jnp.zeros((slot, 128), F32)
        for h in range(2):
            scores = lax.dot_general(source[p, k, h], pk[...], NT, preferred_element_type=F32)
            peak = jnp.max(scores, axis=1, keepdims=True)
            weights = jnp.exp2((scores - peak) * factor)
            total = jnp.sum(weights, axis=1, keepdims=True)
            summed = jnp.dot(weights.astype(BF16), pv[...], preferred_element_type=F32)
            o_to[p, k, h] = (summed / total).astype(BF16)
            stat = jnp.where(lane == 2 * h, peak, jnp.where(lane == 2 * h + 1, total, stat))
        s_to[p, k] = lax.dot_general(
            eye, stat, NT, precision=lax.Precision.HIGHEST, preferred_element_type=F32
        )

    def own_step(p, carry):
        cached(p, 0, q_out, o_in, s_in)
        return carry

    lax.fori_loop(0, pairs, own_step, 0)

    def away(p, k):
        q_copy(p, k).wait_recv()
        cached(p, k, q_in, o_out, s_out)
        s_copy(p, k).start()
        o_copy(p, k).start()

    def away_step(i, carry):
        away(i // (n - 1), i % (n - 1) + 1)
        return carry

    if paired:
        for p in range(pairs):
            for k in order[:-1]:
                away(p, k)
    else:
        lax.fori_loop(0, pairs * (n - 1), away_step, 0)

    for p in range(pairs):
        gathered = jnp.zeros((rows, 2 * hd), F32)
        stat = jnp.zeros((rows, 8), F32)
        for k in order[-1:] + order[:-1]:
            if k:
                s_copy(p, k).wait_recv()
                o_copy(p, k).wait_recv()
            base = target_of(k) * slot
            hot = lax.broadcasted_iota(jnp.int32, (rows, slot), 1) + base == target_col
            block = jnp.concatenate([o_in[p, k, 0], o_in[p, k, 1]], axis=1)
            gathered += jnp.dot(hot.astype(BF16), block, preferred_element_type=F32)
            stat += lax.dot_general(
                hot.astype(F32),
                s_in[p, k],
                NT,
                precision=lax.Precision.HIGHEST,
                preferred_element_type=F32,
            )
        for h in range(2):
            head = 2 * p + h
            peak, total = stat[:, 2 * h : 2 * h + 1], stat[:, 2 * h + 1 : 2 * h + 2]
            own_peak, own_total = own_stat[head][:, 0:1], own_stat[head][:, 1:2]
            top = jnp.maximum(peak, own_peak)
            far = jnp.exp2((peak - top) * factor) * total
            near = jnp.exp2((own_peak - top) * factor)
            mixed = gathered[:, h * hd : (h + 1) * hd] * far + own_acc[head] * near
            out_ref[:, head * hd : (head + 1) * hd] = (
                mixed / (far + near * own_total)
            ).astype(BF16)

    for p in range(pairs):
        for k in range(1, n):
            q_copy(p, k).wait_send()
            o_copy(p, k).wait_send()
            s_copy(p, k).wait_send()


def local(
    hidden,
    lengths,
    assignment,
    norm_gain,
    q_weight,
    q_bias,
    k_weight,
    k_bias,
    v_weight,
    v_bias,
    prompt_keys,
    prompt_values,
):
    n = lax.axis_size("dp")
    rows, feats = hidden.shape
    slot = 2 * rows // n
    hd = k_weight.shape[1]
    cols = q_weight.shape[1]
    pairs = cols // hd // 2
    plen = prompt_keys.shape[0]
    half = hd // 2
    freqs = rope_base ** (-(jnp.arange(half, dtype=F32) * 2.0) / hd)
    position = plen + jnp.arange(slot, dtype=jnp.int32)
    angles = position.astype(F32)[:, None] * freqs[None, :]
    smem = pl.BlockSpec(memory_space=pltpu.SMEM)
    vmem = pl.BlockSpec(memory_space=pltpu.VMEM)
    hbm = pl.BlockSpec(memory_space=pl.ANY)
    dma = pltpu.SemaphoreType.DMA
    flops = 2 * rows * feats * (cols + 2 * hd) + 8 * rows * cols * plen
    return pl.pallas_call(
        functools.partial(kernel, n),
        out_shape=jax.ShapeDtypeStruct((rows, cols), BF16),
        in_specs=[smem, smem, hbm, vmem, hbm, vmem, hbm, vmem, hbm, vmem, hbm, hbm, vmem, vmem],
        out_specs=vmem,
        scratch_shapes=[
            pltpu.VMEM((rows, feats), BF16),
            pltpu.VMEM((rows, feats), BF16),
            pltpu.VMEM((feats, cols), BF16),
            pltpu.VMEM((2, feats, hd), BF16),
            pltpu.VMEM((plen, hd), BF16),
            pltpu.VMEM((plen, hd), BF16),
            pltpu.VMEM((2 * pairs, rows, hd), BF16),
            pltpu.VMEM((pairs, n, 2, slot, hd), BF16),
            pltpu.VMEM((pairs, n, 2, slot, hd), BF16),
            pltpu.VMEM((pairs, n, 2, slot, hd), BF16),
            pltpu.VMEM((pairs, n, 2, slot, hd), BF16),
            pltpu.VMEM((pairs, n, 8, slot), F32),
            pltpu.VMEM((pairs, n, 8, slot), F32),
            pltpu.VMEM((2 * pairs, rows, hd), F32),
            pltpu.VMEM((2 * pairs, rows, 128), F32),
            dma((4,)),
            dma((max(1, rows // min(128, rows)),)),
            dma((pairs,)),
            dma((pairs, n)),
            dma((pairs, n)),
            dma((pairs, n)),
            dma((pairs, n)),
            dma((pairs, n)),
            dma((pairs, n)),
        ],
        compiler_params=pltpu.CompilerParams(
            collective_id=0, has_side_effects=True, vmem_limit_bytes=56 * 1024 * 1024
        ),
        cost_estimate=pl.CostEstimate(
            flops=flops, bytes_accessed=rows * feats * 6, transcendentals=2 * rows * plen * 4
        ),
    )(
        lengths,
        assignment,
        hidden,
        norm_gain,
        q_weight,
        q_bias,
        k_weight,
        k_bias,
        v_weight,
        v_bias,
        prompt_keys,
        prompt_values,
        jnp.cos(angles),
        jnp.sin(angles),
    )


def solution(mesh):
    in_specs = (
        P(("group", "dp"), None),
        P(("group", "dp")),
        P(("group", "dp")),
        P(),
        P(None, "tensor"),
        P("tensor"),
        P(None, "tensor"),
        P("tensor"),
        P(None, "tensor"),
        P("tensor"),
        P(("group", "dp"), "tensor"),
        P(("group", "dp"), "tensor"),
    )
    out_specs = P(("group", "dp"), "tensor")
    return jax.shard_map(
        local, mesh=mesh, in_specs=in_specs, out_specs=out_specs, check_vma=False
    )
```

```python
import functools
import math

import jax
import jax.numpy as jnp
from jax import lax
from jax.experimental import pallas as pl
from jax.experimental.pallas import tpu as pltpu
from jax.sharding import PartitionSpec as P

rope_base = 1000000.0
norm_eps = 1e-06
F32, BF16 = jnp.float32, jnp.bfloat16
MESH = pl.DeviceIdType.MESH
NT = (((1,), (1,)), ((), ()))


def kernel(
    n,
    len_ref,
    dest_ref,
    hidden_hbm,
    gain_ref,
    qw_hbm,
    qb_ref,
    kw_hbm,
    kb_ref,
    vw_hbm,
    vb_ref,
    pk_hbm,
    pv_hbm,
    cos_ref,
    sin_ref,
    out_ref,
    hidden,
    normed,
    qw,
    kvw,
    pk,
    pv,
    queries,
    q_out,
    q_in,
    o_out,
    o_in,
    s_out,
    s_in,
    own_acc,
    own_stat,
    load_sem,
    hidden_sem,
    qw_sem,
    q_send,
    q_recv,
    o_send,
    o_recv,
    s_send,
    s_recv,
):
    rows, feats = hidden.shape
    pairs, _, _, slot, hd = q_out.shape
    responses = len_ref.shape[0]
    factor = hd**-0.5 * math.log2(math.e)
    me = lax.axis_index("dp")

    chunk = min(128, rows)
    chunks = [slice(c * chunk, (c + 1) * chunk) for c in range(rows // chunk)]
    hidden_loads = [
        pltpu.make_async_copy(hidden_hbm.at[at], hidden.at[at], hidden_sem.at[c])
        for c, at in enumerate(chunks)
    ]
    pair_cols = [slice(p * 2 * hd, (p + 1) * 2 * hd) for p in range(pairs)]
    qw_loads = [
        pltpu.make_async_copy(qw_hbm.at[:, at], qw.at[:, at], qw_sem.at[p])
        for p, at in enumerate(pair_cols)
    ]
    loads = qw_loads[1:] + [
        pltpu.make_async_copy(kw_hbm, kvw.at[0], load_sem.at[0]),
        pltpu.make_async_copy(vw_hbm, kvw.at[1], load_sem.at[1]),
        pltpu.make_async_copy(pk_hbm, pk, load_sem.at[2]),
        pltpu.make_async_copy(pv_hbm, pv, load_sem.at[3]),
    ]
    for load in hidden_loads + qw_loads[:1]:
        load.start()

    barrier = pltpu.get_barrier_semaphore()
    for k in range(1, n):
        pl.semaphore_signal(
            barrier, inc=1, device_id={"dp": lax.rem(me + k, n)}, device_id_type=MESH
        )

    paired = n & (n - 1) == 0 and n <= 4

    def toggled(k):
        index = me
        for bit in (1, 2):
            if k & bit:
                index = index + bit - 2 * bit * ((me // bit) % 2)
        return index

    def target_of(k):
        return toggled(k) if paired else lax.rem(me + k, n)

    def origin_of(k):
        return toggled(k) if paired else lax.rem(me - k + n, n)

    lengths = [len_ref[r] for r in range(responses)]
    dests = [dest_ref[r] for r in range(responses)]
    starts, shifts = [], []
    start = jnp.int32(0)
    for r in range(responses):
        offset = jnp.int32(0)
        for e in range(r):
            offset = offset + jnp.where(dests[e] == dests[r], lengths[e], 0)
        starts.append(start)
        shifts.append(dests[r] * slot + offset - start)
        start = start + lengths[r]

    def route(index):
        first = jnp.zeros_like(index)
        shift = jnp.zeros_like(index)
        for r in range(responses):
            reached = index >= starts[r]
            first = jnp.where(reached, starts[r], first)
            shift = jnp.where(reached, shifts[r], shift)
        return first, index + shift

    row_col = lax.broadcasted_iota(jnp.int32, (rows, 1), 0)
    first_col, target_col = route(row_col)
    _, target_row = route(lax.broadcasted_iota(jnp.int32, (1, rows), 1))

    spans = cos_ref.shape[0]
    place_hot = (
        lax.broadcasted_iota(jnp.int32, (rows, spans), 1) == row_col - first_col
    ).astype(F32)
    def turn(ref):
        return jnp.dot(
            place_hot, ref[...], precision=lax.Precision.HIGHEST, preferred_element_type=F32
        )

    cos_half, sin_half = turn(cos_ref), turn(sin_ref)
    cosine = jnp.concatenate([cos_half, cos_half], axis=1)
    sine = jnp.concatenate([-sin_half, sin_half], axis=1)

    def rope(block):
        return (block * cosine + pltpu.roll(block, hd // 2, 1) * sine).astype(BF16)

    gain = gain_ref[...].astype(F32).reshape(1, feats)
    q_bias = qb_ref[...].astype(F32).reshape(1, 2 * pairs * hd)
    k_bias = kb_ref[...].astype(F32).reshape(1, hd)
    v_bias = vb_ref[...].astype(F32).reshape(1, hd)
    first_lin = []
    for c, at in enumerate(chunks):
        hidden_loads[c].wait()
        wide = hidden[at, :].astype(F32)
        scale = lax.rsqrt(jnp.mean(wide * wide, axis=1, keepdims=True) + norm_eps)
        normed[at, :] = (wide * scale * gain).astype(BF16)
        if c == 0:
            qw_loads[0].wait()
        first_lin.append(
            jnp.dot(normed[at, :], qw[:, pair_cols[0]], preferred_element_type=F32)
        )
    for load in loads:
        load.start()

    def q_copy(p, k):
        return pltpu.make_async_remote_copy(
            src_ref=q_out.at[p, k],
            dst_ref=q_in.at[p, k],
            send_sem=q_send.at[p, k],
            recv_sem=q_recv.at[p, k],
            device_id={"dp": target_of(k)},
            device_id_type=MESH,
        )

    def o_copy(p, k):
        return pltpu.make_async_remote_copy(
            src_ref=o_out.at[p, k],
            dst_ref=o_in.at[p, k],
            send_sem=o_send.at[p, k],
            recv_sem=o_recv.at[p, k],
            device_id={"dp": origin_of(k)},
            device_id_type=MESH,
        )

    def s_copy(p, k):
        return pltpu.make_async_remote_copy(
            src_ref=s_out.at[p, k],
            dst_ref=s_in.at[p, k],
            send_sem=s_send.at[p, k],
            recv_sem=s_recv.at[p, k],
            device_id={"dp": origin_of(k)},
            device_id_type=MESH,
        )

    order = ([2, 3, 1] if paired and n == 4 else list(range(1, n))) + [0]
    for p in range(pairs):
        cols = pair_cols[p]
        if p:
            qw_loads[p].wait()
            lin = jnp.dot(normed[...], qw[:, cols], preferred_element_type=F32)
        else:
            lin = jnp.concatenate(first_lin, axis=0)
        lin = lin + q_bias[:, cols]
        both = jnp.concatenate([rope(lin[:, :hd]), rope(lin[:, hd:])], axis=1)
        queries[2 * p] = both[:, :hd]
        queries[2 * p + 1] = both[:, hd:]
        if p == 0:
            pl.semaphore_wait(barrier, n - 1)
        for k in order:
            base = target_of(k) * slot
            hot = lax.broadcasted_iota(jnp.int32, (slot, rows), 0) + base == target_row
            sent = jnp.dot(hot.astype(BF16), both, preferred_element_type=F32).astype(BF16)
            q_out[p, k, 0] = sent[:, :hd]
            q_out[p, k, 1] = sent[:, hd:]
            if k:
                q_copy(p, k).start()

    loads = loads[pairs - 1 :]
    loads[0].wait()
    loads[1].wait()
    k_lin = jnp.dot(normed[...], kvw[0], preferred_element_type=F32) + k_bias
    keys = rope(k_lin)
    v_lin = jnp.dot(normed[...], kvw[1], preferred_element_type=F32) + v_bias
    values = v_lin.astype(BF16)
    col_row = lax.broadcasted_iota(jnp.int32, (rows, rows), 1)
    allowed = (col_row >= first_col) & (col_row <= row_col)
    stat_lane = lax.broadcasted_iota(jnp.int32, (rows, 128), 1)
    for h in range(2 * pairs):
        scores = lax.dot_general(queries[h], keys, NT, preferred_element_type=F32)
        scores = jnp.where(allowed, scores, -jnp.inf)
        peak = jnp.max(scores, axis=1, keepdims=True)
        weights = jnp.exp2((scores - peak) * factor)
        total = jnp.sum(weights, axis=1, keepdims=True)
        own_acc[h] = jnp.dot(weights.astype(BF16), values, preferred_element_type=F32)
        own_stat[h] = jnp.where(stat_lane == 0, peak, total)

    loads[2].wait()
    loads[3].wait()
    eye = (
        lax.broadcasted_iota(jnp.int32, (8, 128), 0) == lax.broadcasted_iota(jnp.int32, (8, 128), 1)
    ).astype(F32)
    lane = lax.broadcasted_iota(jnp.int32, (slot, 128), 1)

    def cached(p, k, source, o_to, s_to):
        stat = jnp.zeros((slot, 128), F32)
        for h in range(2):
            scores = lax.dot_general(source[p, k, h], pk[...], NT, preferred_element_type=F32)
            peak = jnp.max(scores, axis=1, keepdims=True)
            weights = jnp.exp2((scores - peak) * factor)
            total = jnp.sum(weights, axis=1, keepdims=True)
            summed = jnp.dot(weights.astype(BF16), pv[...], preferred_element_type=F32)
            o_to[p, k, h] = (summed / total).astype(BF16)
            stat = jnp.where(lane == 2 * h, peak, jnp.where(lane == 2 * h + 1, total, stat))
        s_to[p, k] = lax.dot_general(
            eye, stat, NT, precision=lax.Precision.HIGHEST, preferred_element_type=F32
        )

    def own_step(p, carry):
        cached(p, 0, q_out, o_in, s_in)
        return carry

    lax.fori_loop(0, pairs, own_step, 0)

    def away(p, k):
        q_copy(p, k).wait_recv()
        cached(p, k, q_in, o_out, s_out)
        s_copy(p, k).start()
        o_copy(p, k).start()

    def away_step(i, carry):
        away(i // (n - 1), i % (n - 1) + 1)
        return carry

    if paired:
        for p in range(pairs):
            for k in order[:-1]:
                away(p, k)
    else:
        lax.fori_loop(0, pairs * (n - 1), away_step, 0)

    def home_hot(k):
        slots = lax.broadcasted_iota(jnp.int32, (rows, slot), 1) + target_of(k) * slot
        return slots == target_col

    for p in range(pairs):
        stat = jnp.zeros((rows, 8), F32)
        for k in order[::-1]:
            if k:
                s_copy(p, k).wait_recv()
            stat += lax.dot_general(
                home_hot(k).astype(F32),
                s_in[p, k],
                NT,
                precision=lax.Precision.HIGHEST,
                preferred_element_type=F32,
            )
        shares, rests = [], []
        for h in range(2):
            head = 2 * p + h
            peak, total = stat[:, 2 * h : 2 * h + 1], stat[:, 2 * h + 1 : 2 * h + 2]
            own_peak, own_total = own_stat[head][:, 0:1], own_stat[head][:, 1:2]
            top = jnp.maximum(peak, own_peak)
            far = jnp.exp2((peak - top) * factor) * total
            near = jnp.exp2((own_peak - top) * factor)
            whole = far + near * own_total
            shares.append(jnp.broadcast_to(far / whole, (rows, hd)))
            rests.append(own_acc[head] * (near / whole))
        gathered = jnp.zeros((rows, 2 * hd), F32)
        for k in order[-1:] + order[-2::-1][:1] + order[:-2]:
            if k:
                o_copy(p, k).wait_recv()
            block = jnp.concatenate([o_in[p, k, 0], o_in[p, k, 1]], axis=1)
            gathered += jnp.dot(home_hot(k).astype(BF16), block, preferred_element_type=F32)
        for h in range(2):
            head = 2 * p + h
            out_ref[:, head * hd : (head + 1) * hd] = (
                gathered[:, h * hd : (h + 1) * hd] * shares[h] + rests[h]
            ).astype(BF16)

    for p in range(pairs):
        for k in range(1, n):
            q_copy(p, k).wait_send()
            o_copy(p, k).wait_send()
            s_copy(p, k).wait_send()


def local(
    hidden,
    lengths,
    assignment,
    norm_gain,
    q_weight,
    q_bias,
    k_weight,
    k_bias,
    v_weight,
    v_bias,
    prompt_keys,
    prompt_values,
):
    n = lax.axis_size("dp")
    rows, feats = hidden.shape
    slot = 2 * rows // n
    hd = k_weight.shape[1]
    cols = q_weight.shape[1]
    pairs = cols // hd // 2
    plen = prompt_keys.shape[0]
    half = hd // 2
    freqs = rope_base ** (-(jnp.arange(half, dtype=F32) * 2.0) / hd)
    position = plen + jnp.arange(slot, dtype=jnp.int32)
    angles = position.astype(F32)[:, None] * freqs[None, :]
    smem = pl.BlockSpec(memory_space=pltpu.SMEM)
    vmem = pl.BlockSpec(memory_space=pltpu.VMEM)
    hbm = pl.BlockSpec(memory_space=pl.ANY)
    dma = pltpu.SemaphoreType.DMA
    flops = 2 * rows * feats * (cols + 2 * hd) + 8 * rows * cols * plen
    return pl.pallas_call(
        functools.partial(kernel, n),
        out_shape=jax.ShapeDtypeStruct((rows, cols), BF16),
        in_specs=[smem, smem, hbm, vmem, hbm, vmem, hbm, vmem, hbm, vmem, hbm, hbm, vmem, vmem],
        out_specs=vmem,
        scratch_shapes=[
            pltpu.VMEM((rows, feats), BF16),
            pltpu.VMEM((rows, feats), BF16),
            pltpu.VMEM((feats, cols), BF16),
            pltpu.VMEM((2, feats, hd), BF16),
            pltpu.VMEM((plen, hd), BF16),
            pltpu.VMEM((plen, hd), BF16),
            pltpu.VMEM((2 * pairs, rows, hd), BF16),
            pltpu.VMEM((pairs, n, 2, slot, hd), BF16),
            pltpu.VMEM((pairs, n, 2, slot, hd), BF16),
            pltpu.VMEM((pairs, n, 2, slot, hd), BF16),
            pltpu.VMEM((pairs, n, 2, slot, hd), BF16),
            pltpu.VMEM((pairs, n, 8, slot), F32),
            pltpu.VMEM((pairs, n, 8, slot), F32),
            pltpu.VMEM((2 * pairs, rows, hd), F32),
            pltpu.VMEM((2 * pairs, rows, 128), F32),
            dma((4,)),
            dma((max(1, rows // min(128, rows)),)),
            dma((pairs,)),
            dma((pairs, n)),
            dma((pairs, n)),
            dma((pairs, n)),
            dma((pairs, n)),
            dma((pairs, n)),
            dma((pairs, n)),
        ],
        compiler_params=pltpu.CompilerParams(
            collective_id=0, has_side_effects=True, vmem_limit_bytes=56 * 1024 * 1024
        ),
        cost_estimate=pl.CostEstimate(
            flops=flops, bytes_accessed=rows * feats * 6, transcendentals=2 * rows * plen * 4
        ),
    )(
        lengths,
        assignment,
        hidden,
        norm_gain,
        q_weight,
        q_bias,
        k_weight,
        k_bias,
        v_weight,
        v_bias,
        prompt_keys,
        prompt_values,
        jnp.cos(angles),
        jnp.sin(angles),
    )


def solution(mesh):
    in_specs = (
        P(("group", "dp"), None),
        P(("group", "dp")),
        P(("group", "dp")),
        P(),
        P(None, "tensor"),
        P("tensor"),
        P(None, "tensor"),
        P("tensor"),
        P(None, "tensor"),
        P("tensor"),
        P(("group", "dp"), "tensor"),
        P(("group", "dp"), "tensor"),
    )
    out_specs = P(("group", "dp"), "tensor")
    return jax.shard_map(
        local, mesh=mesh, in_specs=in_specs, out_specs=out_specs, check_vma=False
    )
```
